32 devices in a mesh: ctx: 8 (over y, x, core), seq: 4 (over z).
Axes of the slice: x: 2, y: 2, z: 4, core: 2. Of those that a mesh axis runs over, the one named last changes fastest.
Arguments:
- lin_query: bfloat16 [2048, 4096], P(('seq', 'ctx')), parts along dimension 0, may hold values from -6 to 6
- lin_keys: bfloat16 [2048, 1024], P(('seq', 'ctx')), parts along dimension 0, may hold values from -6 to 6
- lin_values: bfloat16 [2048, 1024], P(('seq', 'ctx')), parts along dimension 0, may hold values from -6 to 6
- state_in: float32 [32, 128, 128], P('seq'), parts along dimension 0, may hold values from -256 to 256
- norm_gain: float32 [4096], replicated, may hold values from 0.1 to 1.9
- soft_query: bfloat16 [2048, 4096], P(('seq', 'ctx')), parts along dimension 0, may hold values from -7 to 7
- soft_keys: bfloat16 [2048, 1024], P(('seq', 'ctx')), parts along dimension 0, may hold values from -7 to 7
- soft_values: bfloat16 [2048, 1024], P(('seq', 'ctx')), parts along dimension 0, may hold values from -6 to 6
Outputs:
- lin_out: bfloat16 [2048, 4096], P(('seq', 'ctx')), parts along dimension 0
- state_out: float32 [32, 128, 128], P('seq'), parts along dimension 0
- soft_out: bfloat16 [2048, 4096], P(('seq', 'ctx')), parts along dimension 0
The draws below stay inside these ranges and needn't reach their ends.
There are 4 independent parts, one for each index of `seq`. The reference program is written for one: setup_inputs(seed, part) draws one part's arguments, and reference() takes and returns one part's arrays. A program takes and returns all parts, laid end to end along the dimension named above; an argument that names none is the same for every part. Nothing has to cross between parts.
All inputs are finite; a program needn't handle non-finite values.
Results may differ from the reference program's by a relative error of at most 0.014.
Values may be sent and summed in bfloat16 or wider, within the bound.
A program may use at most 64 MiB of HBM per device.

```python
import jax
import jax.numpy as jnp
from jax import lax

H = 32
KVH = 8
HD = 128
D = 4096
KVD = 1024
GROUP = 4
TOK_DEV = 64
TOKENS = 512


def drawn_pair(key):
    query = jax.random.truncated_normal(jax.random.fold_in(key, 11), -6.0, 6.0, (TOKENS, D), jnp.float32)
    keys = jax.random.truncated_normal(jax.random.fold_in(key, 12), -6.0, 6.0, (TOKENS, KVD), jnp.float32)
    return (query, keys)


def draw_soft_query(key, part):
    return drawn_pair(key)[0].astype(jnp.bfloat16)


def draw_soft_keys(key, part):
    return drawn_pair(key)[1].astype(jnp.bfloat16)


def block_scale(stream_key, extent, shards, least, high):
    level = 1.0
    for position, shards_of in shards:
        steps = jax.random.uniform(jax.random.fold_in(jax.random.fold_in(stream_key, 6), position), (shards_of,), jnp.float32, least / len(shards), high / len(shards))
        level = level * jnp.repeat(jnp.exp(steps), extent[position] // shards_of).reshape((-1,) + (1,) * (len(extent) - 1 - position))
    return level


def gaussian(rng, shape, deviation, most, cuts=(), kind=jnp.bfloat16):
    entries = deviation * jax.random.normal(rng, shape, jnp.float32)
    if cuts:
        entries = entries * block_scale(rng, shape, cuts, -0.22, 0.18)
    return jnp.clip(entries, -most, most).astype(kind)


def setup_inputs(seed: int = 0, part: int = 0) -> dict:
    arg_keys = jax.random.split(jax.random.key(seed), 9)
    own_keys = jax.random.split(jax.random.fold_in(arg_keys[8], part), 9)
    return {
        "lin_query": gaussian(own_keys[0], (TOKENS, D), 1.0, 6.0, ((0, 8),)),
        "lin_keys": gaussian(own_keys[1], (TOKENS, KVD), 1.0, 6.0, ((0, 8),)),
        "lin_values": gaussian(own_keys[2], (TOKENS, KVD), 1.0, 6.0, ((0, 8),)),
        "state_in": gaussian(own_keys[3], (KVH, HD, HD), (TOK_DEV // 2 + 8), 256.0, (), jnp.float32),
        "norm_gain": jnp.clip(1.0 + 0.18 * jax.random.normal(arg_keys[4], (D,), jnp.float32), 0.1, 1.9),
        "soft_query": draw_soft_query(jax.random.fold_in(jax.random.fold_in(arg_keys[8], part), 71), part),
        "soft_keys": draw_soft_keys(jax.random.fold_in(jax.random.fold_in(arg_keys[8], part), 71), part),
        "soft_values": gaussian(own_keys[7], (TOKENS, KVD), 1.0, 6.0, ((0, 8),)),
    }


def linear_blocks(query, keys, values, state):
    total = query.shape[0]
    block = min(512, total)
    steps = total // block
    heads = query.shape[1]
    width = query.shape[2]
    q_blocks = query.reshape(steps, block, heads, width)
    k_blocks = keys.reshape(steps, block, heads, width)
    v_blocks = values.reshape(steps, block, heads, width)
    lower = jnp.tril(jnp.ones((block, block), jnp.float32))

    def advance(memory, pieces):
        q_block, k_block, v_block = pieces
        carried = jnp.einsum('thd,hde->the', q_block.astype(jnp.float32), memory, precision=lax.Precision.HIGHEST)
        inner_scores = jnp.einsum('thd,shd->hts', q_block, k_block, preferred_element_type=jnp.float32) * lower
        inner = jnp.einsum('hts,she->the', inner_scores, v_block.astype(jnp.float32), precision=lax.Precision.HIGHEST)
        update = jnp.einsum('thd,the->hde', k_block, v_block, preferred_element_type=jnp.float32)
        return (memory + update, carried + inner)
    final, outputs = lax.scan(advance, state, (q_blocks, k_blocks, v_blocks))
    return (outputs.reshape(total, heads, width), final)

def head_norm(raw, gain):
    square = lax.optimization_barrier(jnp.mean(raw * raw, axis=-1, keepdims=True))
    return (raw * lax.rsqrt(square + 1e-06) * gain).astype(jnp.bfloat16)

def causal_softmax(query, keys, values):
    total = query.shape[0]
    heads = query.shape[1]
    width = query.shape[2]
    block = min(512, total)
    steps = total // block
    scale = width ** (-0.5)
    q_blocks = query.reshape(steps, block, heads, width)
    key_pos = jnp.arange(total, dtype=jnp.int32)

    def one_block(pieces):
        q_block, offset = pieces
        scores = jnp.einsum('qmd,kmd->mqk', q_block, keys, preferred_element_type=jnp.float32) * scale
        query_pos = offset + jnp.arange(block, dtype=jnp.int32)
        allowed = key_pos[None, None, :] <= query_pos[None, :, None]
        scores = jnp.where(allowed, scores, -1e+30)
        top = lax.optimization_barrier(jnp.max(scores, axis=-1, keepdims=True))
        expo = jnp.exp(scores - top)
        weights = (expo / lax.optimization_barrier(jnp.sum(expo, axis=-1, keepdims=True))).astype(jnp.bfloat16)
        return jnp.einsum('mqk,kmd->qmd', weights, values, preferred_element_type=jnp.float32).astype(jnp.bfloat16)
    offsets = (jnp.arange(steps, dtype=jnp.int32) * block).astype(jnp.int32)
    outputs = lax.map(one_block, (q_blocks, offsets))
    return outputs.reshape(total, heads, width)

def expand(shared):
    return jnp.repeat(shared.reshape(TOKENS, KVH, HD), GROUP, axis=1)

def reference(lin_query, lin_keys, lin_values, state_in, norm_gain, soft_query, soft_keys, soft_values):
    split = (TOKENS, H, HD)
    start = jnp.repeat(state_in, GROUP, axis=0)
    raw, final = linear_blocks(lin_query.reshape(split), expand(lin_keys), expand(lin_values), start)
    lin_out = head_norm(raw, norm_gain.reshape(H, HD)).reshape(TOKENS, D)
    state_out = final.reshape(KVH, GROUP, HD, HD)[:, 0]
    soft_input = (soft_query.astype(jnp.float32) + lin_out.astype(jnp.float32)).astype(jnp.bfloat16)
    soft_out = causal_softmax(soft_input.reshape(split), expand(soft_keys), expand(soft_values)).reshape(TOKENS, D)
    return (lin_out, state_out, soft_out)
```

```python
import functools

import jax
import jax.numpy as jnp
from jax import lax
from jax.experimental import pallas as pl
from jax.experimental.pallas import tpu as pltpu
from jax.sharding import PartitionSpec as P

F32 = jnp.float32
BF16 = jnp.bfloat16
LOG2E = 1.4426950408889634


def dot(a, b, dims=((1,), (0,))):
    return lax.dot_general(a, b, (dims, ((), ())), preferred_element_type=F32)


def kernel(
    n, group, width,
    lq_h, lk_h, lv_h, st_h, gain, sq_h, sk_h, sv_h,
    lo_o, st_o, so_o,
    lq, lk, lv, sq, sk, sv, stin, stall, total, raw, qs, ob, out, top, acc,
    loc, pair_s, pair_r, soft_s, soft_r, st_s, st_r, out_s, out_r, out_l,
):
    me = lax.axis_index("ctx")
    c, r = me // 2, me % 2
    sib = 2 * c + 1 - r
    chips = n // 2
    T = lk_h.shape[0]
    T2 = 2 * T
    KW = lk.shape[1]
    QW = lq.shape[1]
    G = KW // width
    R = group * T2

    barrier = pltpu.get_barrier_semaphore()
    for k in range(1, n):
        pl.semaphore_signal(barrier, inc=1, device_id={"ctx": lax.rem(me + k, n)},
                            device_id_type=pl.DeviceIdType.MESH)
    pl.semaphore_wait(barrier, n - 1)

    def rows(d):
        return pl.ds(pl.multiple_of(d * T, T), T)

    def cols(h, w):
        return pl.ds(pl.multiple_of(h * w, w), w)

    def remote(src, dst, ss, rs, dev):
        return pltpu.make_async_remote_copy(
            src_ref=src, dst_ref=dst, send_sem=ss, recv_sem=rs,
            device_id={"ctx": dev}, device_id_type=pl.DeviceIdType.MESH)

    pair = []
    for i, (src, dst, w) in enumerate(((lk_h, lk, KW), (lv_h, lv, KW), (lq_h, lq, QW), (sq_h, sq, QW))):
        cp = remote(src.at[:, cols(1 - r, w)], dst.at[rows(r)], pair_s.at[i], pair_r.at[i], sib)
        cp.start()
        lc = pltpu.make_async_copy(src.at[:, cols(r, w)], dst.at[rows(r)], loc.at[i])
        lc.start()
        rc = remote(src.at[:, cols(r, w)], dst.at[rows(1 - r)], pair_s.at[i], pair_r.at[i], sib)
        pair.append((cp, lc, rc))
    lst = pltpu.make_async_copy(st_h.at[pl.ds(r * G, G)], stin, loc.at[4])
    lst.start()

    softs = ((sk_h, sk), (sv_h, sv))
    own = []
    for a, (src, dst) in enumerate(softs):
        lc = pltpu.make_async_copy(src.at[:, cols(r, KW)], dst.at[rows(me)], loc.at[5 + a])
        lc.start()
        own.append(lc)
        cp = remote(src.at[:, cols(1 - r, KW)], dst.at[rows(me)], soft_s.at[a, sib], soft_r.at[a, me], sib)
        cp.start()

    def soft_send(a, dest, h):
        src, dst = softs[a]
        return remote(src.at[:, h * KW:(h + 1) * KW], dst.at[rows(me)], soft_s.at[a, dest],
                      soft_r.at[a, me], dest)

    def soft_wait(d):
        for a, (src, dst) in enumerate(softs):
            remote(src.at[:, 0:KW], dst.at[rows(d)], soft_s.at[a, d], soft_r.at[a, d], sib).wait_recv()

    for k in range(1, chips):
        @pl.when(c + k < chips)
        def _():
            for h in range(2):
                for a in range(2):
                    soft_send(a, 2 * (c + k) + h, h).start()

    for i in range(2):
        pair[i][1].wait()
        pair[i][2].wait_recv()
    for g in range(G):
        s = slice(g * width, (g + 1) * width)
        stall[c, g] = dot(lk[:, s], lv[:, s], ((0,), (0,))).astype(BF16)

    def state_send(k):
        p = lax.rem(c + k, chips)
        return remote(stall.at[c], stall.at[c], st_s.at[p], st_r.at[c], 2 * p + r)

    def state_recv(k):
        p = lax.rem(c + k, chips)
        return remote(stall.at[p], stall.at[p], st_s.at[p], st_r.at[p], 2 * p + r)

    for k in range(1, chips):
        state_send(k).start()

    for i in range(2, 4):
        pair[i][1].wait()
        pair[i][2].wait_recv()
    tok = lax.rem(lax.broadcasted_iota(jnp.int32, (R, T2), 0), T2)
    keep = lax.broadcasted_iota(jnp.int32, (R, T2), 1) <= tok

    def grouped(ref, g):
        return jnp.concatenate(
            [ref[:, (g * group + i) * width:(g * group + i + 1) * width] for i in range(group)], axis=0)

    for g in range(G):
        s = slice(g * width, (g + 1) * width)
        sc = jnp.where(keep, dot(grouped(lq, g), lk[:, s], ((1,), (1,))), 0.0)
        hi = sc.astype(BF16)
        lo = (sc - hi.astype(F32)).astype(BF16)
        raw[g] = dot(hi, lv[:, s]) + dot(lo, lv[:, s])

    lst.wait()
    for k in range(1, chips):
        state_recv(k).wait_recv()
    for g in range(G):
        before = stin[g]
        whole = before
        for p in range(chips):
            x = stall[p, g].astype(F32)
            whole = whole + x
            before = before + jnp.where(p < c, x, 0.0)
        total[g] = whole
        hi = before.astype(BF16)
        lo = (before - hi.astype(F32)).astype(BF16)
        q = grouped(lq, g)
        full = raw[g] + dot(q, hi) + dot(q, lo)
        inv = lax.rsqrt(jnp.mean(full * full, axis=-1, keepdims=True) + 1e-6)
        full = full * inv
        for i in range(group):
            h = g * group + i
            hs = slice(h * width, (h + 1) * width)
            o = (full[i * T2:(i + 1) * T2] * gain[pl.ds(r * (G * group) + h, 1), :]).astype(BF16)
            ob[:, hs] = o
            qs[g, i * T2:(i + 1) * T2, :] = (sq[:, hs].astype(F32) + o.astype(F32)).astype(BF16)

    def outgo(i, src, dst):
        return (remote(src[1], dst, out_s.at[i], out_r.at[i], sib),
                pltpu.make_async_copy(src[0], dst, out_l.at[i]))

    sends = [
        outgo(0, (ob.at[rows(r)], ob.at[rows(1 - r)]), lo_o.at[:, cols(r, QW)]),
        outgo(1, (total, total), st_o.at[pl.ds(r * G, G)]),
    ]
    for cp, lc in sends:
        cp.start()
        lc.start()

    scale = width ** (-0.5) * LOG2E
    ones = jnp.ones((T2, width), BF16)

    for lc in own:
        lc.wait()
    soft_wait(sib)
    mine = pl.ds(pl.multiple_of(c * T2, T2), T2)
    for g in range(G):
        s = slice(g * width, (g + 1) * width)
        sc = jnp.where(keep, dot(qs[g], sk[mine, s], ((1,), (1,))) * scale, -1e30)
        m = jnp.max(sc, axis=-1, keepdims=True)
        e = jnp.exp2(sc - m).astype(BF16)
        acc[g] = dot(e, jnp.concatenate([sv[mine, s], ones], axis=1))
        top[g] = jnp.broadcast_to(m, (R, width))

    def block(j, _):
        p = c - j
        soft_wait(2 * p)
        soft_wait(2 * p + 1)
        at = pl.ds(pl.multiple_of(p * T2, T2), T2)
        for g in range(G):
            s = slice(g * width, (g + 1) * width)
            sc = dot(qs[g], sk[at, s], ((1,), (1,))) * scale
            old = top[g][:, 0:1]
            m = jnp.maximum(old, jnp.max(sc, axis=-1, keepdims=True))
            e = jnp.exp2(sc - m).astype(BF16)
            acc[g] = acc[g] * jnp.exp2(old - m) + dot(e, jnp.concatenate([sv[at, s], ones], axis=1))
            top[g] = jnp.broadcast_to(m, (R, width))
        return 0

    lax.fori_loop(1, c + 1, block, 0)
    for g in range(G):
        o = (acc[g, :, 0:width] / acc[g, :, width:2 * width]).astype(BF16)
        for i in range(group):
            h = g * group + i
            out[:, h * width:(h + 1) * width] = o[i * T2:(i + 1) * T2]
    sends.append(outgo(2, (out.at[rows(r)], out.at[rows(1 - r)]), so_o.at[:, cols(r, QW)]))
    sends[2][0].start()
    sends[2][1].start()

    for cp, _, _ in pair:
        cp.wait_send()
    for a in range(2):
        soft_send(a, sib, 0).wait_send()
    for k in range(1, chips):
        state_send(k).wait_send()

        @pl.when(c + k < chips)
        def _():
            for h in range(2):
                for a in range(2):
                    soft_send(a, 2 * (c + k) + h, h).wait_send()
    other = 1 - r
    lands = (lo_o.at[:, cols(other, QW)], st_o.at[pl.ds(other * G, G)], so_o.at[:, cols(other, QW)])
    for i, (cp, lc) in enumerate(sends):
        cp.wait_send()
        lc.wait()
        src = (ob.at[rows(r)], total, out.at[rows(r)])[i]
        remote(src, lands[i], out_s.at[i], out_r.at[i], sib).wait_recv()


def shards(n, lin_query, lin_keys, lin_values, state_in, norm_gain, soft_query, soft_keys, soft_values):
    T, D = lin_query.shape
    kvh, width, _ = state_in.shape
    kvd = lin_keys.shape[1]
    heads = D // width
    group = heads // kvh
    G = kvh // 2
    R = group * 2 * T
    chips = n // 2
    hbm = pl.BlockSpec(memory_space=pl.ANY)
    dma = pltpu.SemaphoreType.DMA
    return pl.pallas_call(
        functools.partial(kernel, n, group, width),
        out_shape=(
            jax.ShapeDtypeStruct((T, D), BF16),
            jax.ShapeDtypeStruct(state_in.shape, F32),
            jax.ShapeDtypeStruct((T, D), BF16),
        ),
        in_specs=[hbm, hbm, hbm, hbm, pl.BlockSpec(memory_space=pltpu.VMEM), hbm, hbm, hbm],
        out_specs=(hbm, hbm, hbm),
        scratch_shapes=[
            pltpu.VMEM((2 * T, D // 2), BF16),
            pltpu.VMEM((2 * T, kvd // 2), BF16),
            pltpu.VMEM((2 * T, kvd // 2), BF16),
            pltpu.VMEM((2 * T, D // 2), BF16),
            pltpu.VMEM((n * T, kvd // 2), BF16),
            pltpu.VMEM((n * T, kvd // 2), BF16),
            pltpu.VMEM((G, width, width), F32),
            pltpu.VMEM((chips, G, width, width), BF16),
            pltpu.VMEM((G, width, width), F32),
            pltpu.VMEM((G, R, width), F32),
            pltpu.VMEM((G, R, width), BF16),
            pltpu.VMEM((2 * T, D // 2), BF16),
            pltpu.VMEM((2 * T, D // 2), BF16),
            pltpu.VMEM((G, R, width), F32),
            pltpu.VMEM((G, R, 2 * width), F32),
            dma((7,)), dma((4,)), dma((4,)), dma((2, n)), dma((2, n)),
            dma((chips,)), dma((chips,)), dma((3,)), dma((3,)), dma((3,)),
        ],
        compiler_params=pltpu.CompilerParams(
            collective_id=0, has_side_effects=True, vmem_limit_bytes=48 * 1024 * 1024),
        cost_estimate=pl.CostEstimate(flops=2_000_000_000, bytes_accessed=8_000_000, transcendentals=1_000_000),
    )(lin_query, lin_keys, lin_values, state_in, norm_gain.reshape(heads, width),
      soft_query, soft_keys, soft_values)


def solution(mesh):
    tok = P(("seq", "ctx"), None)
    st = P("seq", None, None)
    return jax.shard_map(
        functools.partial(shards, mesh.shape["ctx"]), mesh=mesh,
        in_specs=(tok, tok, tok, st, P(), tok, tok, tok),
        out_specs=(tok, st, tok), check_vma=False)
```

```python
import functools

import jax
import jax.numpy as jnp
from jax import lax
from jax.experimental import pallas as pl
from jax.experimental.pallas import tpu as pltpu
from jax.sharding import PartitionSpec as P

F32 = jnp.float32
BF16 = jnp.bfloat16
LOG2E = 1.4426950408889634


def dot(a, b, dims=((1,), (0,))):
    return lax.dot_general(a, b, (dims, ((), ())), preferred_element_type=F32)


def kernel(
    n, group, width,
    lq_h, lk_h, lv_h, st_h, gain_h, sq_h, sk_h, sv_h,
    lo_o, st_o, so_o,
    lq, lk, lv, sq, sk, sv, gain, stin, stall, total, raw, qs, ob, out, top, acc,
    loc, pair_s, pair_r, soft_s, soft_r, st_s, st_r, out_s, out_r, out_l,
):
    me = lax.axis_index("ctx")
    c, r = me // 2, me % 2
    sib = 2 * c + 1 - r
    chips = n // 2
    T = lk_h.shape[0]
    T2 = 2 * T
    KW = lk.shape[1]
    QW = lq.shape[1]
    G = KW // width
    R = group * T2

    barrier = pltpu.get_barrier_semaphore()
    for k in range(1, n):
        pl.semaphore_signal(barrier, inc=1, device_id={"ctx": lax.rem(me + k, n)},
                            device_id_type=pl.DeviceIdType.MESH)
    pl.semaphore_wait(barrier, n - 1)

    def rows(d):
        return pl.ds(pl.multiple_of(d * T, T), T)

    def cols(h, w):
        return pl.ds(pl.multiple_of(h * w, w), w)

    def remote(src, dst, ss, rs, dev):
        return pltpu.make_async_remote_copy(
            src_ref=src, dst_ref=dst, send_sem=ss, recv_sem=rs,
            device_id={"ctx": dev}, device_id_type=pl.DeviceIdType.MESH)

    pair = []
    for i, (src, dst, w) in enumerate(((lk_h, lk, KW), (lv_h, lv, KW), (lq_h, lq, QW), (sq_h, sq, QW))):
        cp = remote(src.at[:, cols(1 - r, w)], dst.at[rows(r)], pair_s.at[i], pair_r.at[i], sib)
        cp.start()
        lc = pltpu.make_async_copy(src.at[:, cols(r, w)], dst.at[rows(r)], loc.at[i])
        lc.start()
        rc = remote(src.at[:, cols(r, w)], dst.at[rows(1 - r)], pair_s.at[i], pair_r.at[i], sib)
        pair.append((cp, lc, rc))
    lst = pltpu.make_async_copy(st_h.at[pl.ds(r * G, G)], stin, loc.at[4])
    lst.start()
    lgain = pltpu.make_async_copy(gain_h, gain, loc.at[7])
    lgain.start()

    softs = ((sk_h, sk), (sv_h, sv))
    own = []
    for a, (src, dst) in enumerate(softs):
        lc = pltpu.make_async_copy(src.at[:, cols(r, KW)], dst.at[rows(me)], loc.at[5 + a])
        lc.start()
        own.append(lc)
        cp = remote(src.at[:, cols(1 - r, KW)], dst.at[rows(me)], soft_s.at[a, sib], soft_r.at[a, me], sib)
        cp.start()

    def soft_send(a, dest, h):
        src, dst = softs[a]
        return remote(src.at[:, h * KW:(h + 1) * KW], dst.at[rows(me)], soft_s.at[a, dest],
                      soft_r.at[a, me], dest)

    def soft_wait(d):
        for a, (src, dst) in enumerate(softs):
            remote(src.at[:, 0:KW], dst.at[rows(d)], soft_s.at[a, d], soft_r.at[a, d], sib).wait_recv()

    for i in range(2):
        pair[i][1].wait()
        pair[i][2].wait_recv()
    for g in range(G):
        s = slice(g * width, (g + 1) * width)
        stall[c, g] = dot(lk[:, s], lv[:, s], ((0,), (0,))).astype(BF16)

    def state_send(k):
        p = lax.rem(c + k, chips)
        return remote(stall.at[c], stall.at[c], st_s.at[p], st_r.at[c], 2 * p + r)

    def state_recv(k):
        p = lax.rem(c + k, chips)
        return remote(stall.at[p], stall.at[p], st_s.at[p], st_r.at[p], 2 * p + r)

    for k in range(1, chips):
        state_send(k).start()
    for k in range(1, chips):
        @pl.when(c + k < chips)
        def _():
            for h in range(2):
                for a in range(2):
                    soft_send(a, 2 * (c + k) + h, h).start()

    for i in range(2, 4):
        pair[i][1].wait()
        pair[i][2].wait_recv()
    tok = lax.rem(lax.broadcasted_iota(jnp.int32, (R, T2), 0), T2)
    keep = lax.broadcasted_iota(jnp.int32, (R, T2), 1) <= tok

    def grouped(ref, g):
        return jnp.concatenate(
            [ref[:, (g * group + i) * width:(g * group + i + 1) * width] for i in range(group)], axis=0)

    for g in range(G):
        s = slice(g * width, (g + 1) * width)
        sc = jnp.where(keep, dot(grouped(lq, g), lk[:, s], ((1,), (1,))), 0.0)
        hi = sc.astype(BF16)
        lo = (sc - hi.astype(F32)).astype(BF16)
        raw[g] = dot(hi, lv[:, s]) + dot(lo, lv[:, s])

    lst.wait()
    lgain.wait()
    for k in range(1, chips):
        state_recv(k).wait_recv()
    for g in range(G):
        before = stin[g]
        whole = before
        for p in range(chips):
            x = stall[p, g].astype(F32)
            whole = whole + x
            before = before + jnp.where(p < c, x, 0.0)
        total[g] = whole
        hi = before.astype(BF16)
        lo = (before - hi.astype(F32)).astype(BF16)
        q = grouped(lq, g)
        full = raw[g] + dot(q, hi) + dot(q, lo)
        inv = lax.rsqrt(jnp.mean(full * full, axis=-1, keepdims=True) + 1e-6)
        full = full * inv
        for i in range(group):
            h = g * group + i
            hs = slice(h * width, (h + 1) * width)
            o = (full[i * T2:(i + 1) * T2] * gain[pl.ds(r * (G * group) + h, 1), :]).astype(BF16)
            ob[:, hs] = o
            qs[g, i * T2:(i + 1) * T2, :] = (sq[:, hs].astype(F32) + o.astype(F32)).astype(BF16)

    def outgo(i, src, dst):
        return (remote(src[1], dst, out_s.at[i], out_r.at[i], sib),
                pltpu.make_async_copy(src[0], dst, out_l.at[i]))

    sends = [
        outgo(0, (ob.at[rows(r)], ob.at[rows(1 - r)]), lo_o.at[:, cols(r, QW)]),
        outgo(1, (total, total), st_o.at[pl.ds(r * G, G)]),
    ]
    for cp, lc in sends:
        cp.start()
        lc.start()

    scale = width ** (-0.5) * LOG2E
    ones = jnp.ones((T2, width), BF16)

    for lc in own:
        lc.wait()
    soft_wait(sib)
    mine = pl.ds(pl.multiple_of(c * T2, T2), T2)
    for g in range(G):
        s = slice(g * width, (g + 1) * width)
        sc = jnp.where(keep, dot(qs[g], sk[mine, s], ((1,), (1,))) * scale, -1e30)
        m = jnp.max(sc, axis=-1, keepdims=True)
        e = jnp.exp2(sc - m).astype(BF16)
        acc[g] = dot(e, jnp.concatenate([sv[mine, s], ones], axis=1))
        top[g] = jnp.broadcast_to(m, (R, width))

    def block(j, _):
        p = c - j
        soft_wait(2 * p)
        soft_wait(2 * p + 1)
        at = pl.ds(pl.multiple_of(p * T2, T2), T2)
        for g in range(G):
            s = slice(g * width, (g + 1) * width)
            sc = dot(qs[g], sk[at, s], ((1,), (1,))) * scale
            old = top[g][:, 0:1]
            m = jnp.maximum(old, jnp.max(sc, axis=-1, keepdims=True))
            e = jnp.exp2(sc - m).astype(BF16)
            acc[g] = acc[g] * jnp.exp2(old - m) + dot(e, jnp.concatenate([sv[at, s], ones], axis=1))
            top[g] = jnp.broadcast_to(m, (R, width))
        return 0

    lax.fori_loop(1, c + 1, block, 0)
    for g in range(G):
        o = (acc[g, :, 0:width] / acc[g, :, width:2 * width]).astype(BF16)
        for i in range(group):
            h = g * group + i
            out[:, h * width:(h + 1) * width] = o[i * T2:(i + 1) * T2]
    sends.append(outgo(2, (out.at[rows(r)], out.at[rows(1 - r)]), so_o.at[:, cols(r, QW)]))
    sends[2][0].start()
    sends[2][1].start()

    for cp, _, _ in pair:
        cp.wait_send()
    for a in range(2):
        soft_send(a, sib, 0).wait_send()
    for k in range(1, chips):
        state_send(k).wait_send()

        @pl.when(c + k < chips)
        def _():
            for h in range(2):
                for a in range(2):
                    soft_send(a, 2 * (c + k) + h, h).wait_send()
    other = 1 - r
    lands = (lo_o.at[:, cols(other, QW)], st_o.at[pl.ds(other * G, G)], so_o.at[:, cols(other, QW)])
    for i, (cp, lc) in enumerate(sends):
        cp.wait_send()
        lc.wait()
        src = (ob.at[rows(r)], total, out.at[rows(r)])[i]
        remote(src, lands[i], out_s.at[i], out_r.at[i], sib).wait_recv()


def deliver(a, b, c, a_o, b_o, c_o):
    a_o[...] = a[...]
    b_o[...] = b[...]
    c_o[...] = c[...]


def shards(n, lin_query, lin_keys, lin_values, state_in, norm_gain, soft_query, soft_keys, soft_values):
    T, D = lin_query.shape
    kvh, width, _ = state_in.shape
    kvd = lin_keys.shape[1]
    heads = D // width
    group = heads // kvh
    G = kvh // 2
    R = group * 2 * T
    chips = n // 2
    hbm = pl.BlockSpec(memory_space=pltpu.HBM)
    near = pl.BlockSpec(memory_space=pl.ANY)
    dma = pltpu.SemaphoreType.DMA
    shapes = (
        jax.ShapeDtypeStruct((T, D), BF16),
        jax.ShapeDtypeStruct(state_in.shape, F32),
        jax.ShapeDtypeStruct((T, D), BF16),
    )
    results = pl.pallas_call(
        functools.partial(kernel, n, group, width),
        out_shape=shapes,
        in_specs=[hbm] * 8,
        out_specs=(near, near, near),
        scratch_shapes=[
            pltpu.VMEM((2 * T, D // 2), BF16),
            pltpu.VMEM((2 * T, kvd // 2), BF16),
            pltpu.VMEM((2 * T, kvd // 2), BF16),
            pltpu.VMEM((2 * T, D // 2), BF16),
            pltpu.VMEM((n * T, kvd // 2), BF16),
            pltpu.VMEM((n * T, kvd // 2), BF16),
            pltpu.VMEM((heads, width), F32),
            pltpu.VMEM((G, width, width), F32),
            pltpu.VMEM((chips, G, width, width), BF16),
            pltpu.VMEM((G, width, width), F32),
            pltpu.VMEM((G, R, width), F32),
            pltpu.VMEM((G, R, width), BF16),
            pltpu.VMEM((2 * T, D // 2), BF16),
            pltpu.VMEM((2 * T, D // 2), BF16),
            pltpu.VMEM((G, R, width), F32),
            pltpu.VMEM((G, R, 2 * width), F32),
            dma((8,)), dma((4,)), dma((4,)), dma((2, n)), dma((2, n)),
            dma((chips,)), dma((chips,)), dma((3,)), dma((3,)), dma((3,)),
        ],
        compiler_params=pltpu.CompilerParams(
            collective_id=0, has_side_effects=True, vmem_limit_bytes=63 * 1024 * 1024),
        cost_estimate=pl.CostEstimate(flops=2_000_000_000, bytes_accessed=8_000_000, transcendentals=1_000_000),
    )(lin_query, lin_keys, lin_values, state_in, norm_gain.reshape(heads, width),
      soft_query, soft_keys, soft_values)
    return pl.pallas_call(
        deliver, out_shape=shapes,
    )(*results)


def solution(mesh):
    tok = P(("seq", "ctx"), None)
    st = P("seq", None, None)
    return jax.shard_map(
        functools.partial(shards, mesh.shape["ctx"]), mesh=mesh,
        in_specs=(tok, tok, tok, st, P(), tok, tok, tok),
        out_specs=(tok, st, tok), check_vma=False)
```

```python
import functools

import jax
import jax.numpy as jnp
from jax import lax
from jax.experimental import pallas as pl
from jax.experimental.pallas import tpu as pltpu
from jax.sharding import PartitionSpec as P

F32 = jnp.float32
BF16 = jnp.bfloat16
LOG2E = 1.4426950408889634


def dot(a, b, dims=((1,), (0,))):
    return lax.dot_general(a, b, (dims, ((), ())), preferred_element_type=F32)


def kernel(
    n, group, width,
    lq_h, lk_h, lv_h, st_h, gain_h, sq_h, sk_h, sv_h,
    lo_o, st_o, so_o,
    lq, lk, lv, sq, sk, sv, gain, stin, stall, total, raw, qs, ob, out, top, acc,
    loc, pair_s, pair_r, soft_s, soft_r, st_s, st_r, out_s, out_r, out_l,
):
    me = lax.axis_index("ctx")
    c, r = me // 2, me % 2
    sib = 2 * c + 1 - r
    chips = n // 2
    T = lk_h.shape[0]
    T2 = 2 * T
    KW = lk.shape[1]
    QW = lq.shape[1]
    G = KW // width
    R = group * T2

    def rows(d):
        return pl.ds(pl.multiple_of(d * T, T), T)

    def cols(h, w):
        return pl.ds(pl.multiple_of(h * w, w), w)

    def remote(src, dst, ss, rs, dev):
        return pltpu.make_async_remote_copy(
            src_ref=src, dst_ref=dst, send_sem=ss, recv_sem=rs,
            device_id={"ctx": dev}, device_id_type=pl.DeviceIdType.MESH)

    streams = ((lk_h, lk, KW), (lv_h, lv, KW), (lq_h, lq, QW), (sq_h, sq, QW))
    softs = ((sk_h, sk), (sv_h, sv))
    near = [pltpu.make_async_copy(src.at[:, cols(r, w)], dst.at[rows(r)], loc.at[i])
            for i, (src, dst, w) in enumerate(streams)]
    own = [pltpu.make_async_copy(src.at[:, cols(r, KW)], dst.at[rows(me)], loc.at[5 + a])
           for a, (src, dst) in enumerate(softs)]
    lst = pltpu.make_async_copy(st_h.at[pl.ds(r * G, G)], stin, loc.at[4])
    lgain = pltpu.make_async_copy(gain_h, gain, loc.at[7])
    for lc in near + own + [lst, lgain]:
        lc.start()

    barrier = pltpu.get_barrier_semaphore()
    for k in range(1, n):
        pl.semaphore_signal(barrier, inc=1, device_id={"ctx": lax.rem(me + k, n)},
                            device_id_type=pl.DeviceIdType.MESH)
    pl.semaphore_wait(barrier, n - 1)

    pair = []
    for i, (src, dst, w) in enumerate(streams):
        cp = remote(src.at[:, cols(1 - r, w)], dst.at[rows(r)], pair_s.at[i], pair_r.at[i], sib)
        cp.start()
        rc = remote(src.at[:, cols(r, w)], dst.at[rows(1 - r)], pair_s.at[i], pair_r.at[i], sib)
        pair.append((cp, near[i], rc))

    for a, (src, dst) in enumerate(softs):
        cp = remote(src.at[:, cols(1 - r, KW)], dst.at[rows(me)], soft_s.at[a, sib], soft_r.at[a, me], sib)
        cp.start()

    def soft_send(a, dest, h):
        src, dst = softs[a]
        return remote(src.at[:, h * KW:(h + 1) * KW], dst.at[rows(me)], soft_s.at[a, dest],
                      soft_r.at[a, me], dest)

    def soft_wait(d):
        for a, (src, dst) in enumerate(softs):
            remote(src.at[:, 0:KW], dst.at[rows(d)], soft_s.at[a, d], soft_r.at[a, d], sib).wait_recv()

    for i in range(2):
        pair[i][1].wait()
        pair[i][2].wait_recv()
    for g in range(G):
        s = slice(g * width, (g + 1) * width)
        stall[c, g] = dot(lk[:, s], lv[:, s], ((0,), (0,))).astype(BF16)

    def state_send(k):
        p = lax.rem(c + k, chips)
        return remote(stall.at[c], stall.at[c], st_s.at[p], st_r.at[c], 2 * p + r)

    def state_recv(k):
        p = lax.rem(c + k, chips)
        return remote(stall.at[p], stall.at[p], st_s.at[p], st_r.at[p], 2 * p + r)

    for k in range(1, chips):
        state_send(k).start()
    for k in range(1, chips):
        @pl.when(c + k < chips)
        def _():
            for h in range(2):
                for a in range(2):
                    soft_send(a, 2 * (c + k) + h, h).start()

    for i in range(2, 4):
        pair[i][1].wait()
        pair[i][2].wait_recv()
    tok = lax.rem(lax.broadcasted_iota(jnp.int32, (R, T2), 0), T2)
    keep = lax.broadcasted_iota(jnp.int32, (R, T2), 1) <= tok

    def grouped(ref, g):
        return jnp.concatenate(
            [ref[:, (g * group + i) * width:(g * group + i + 1) * width] for i in range(group)], axis=0)

    for g in range(G):
        s = slice(g * width, (g + 1) * width)
        sc = jnp.where(keep, dot(grouped(lq, g), lk[:, s], ((1,), (1,))), 0.0)
        hi = sc.astype(BF16)
        lo = (sc - hi.astype(F32)).astype(BF16)
        raw[g] = dot(jnp.concatenate([hi, lo], axis=1), jnp.concatenate([lv[:, s], lv[:, s]], axis=0))

    lst.wait()
    lgain.wait()
    for k in range(1, chips):
        state_recv(k).wait_recv()
    for g in range(G):
        before = stin[g]
        whole = before
        for p in range(chips):
            x = stall[p, g].astype(F32)
            whole = whole + x
            before = before + jnp.where(p < c, x, 0.0)
        total[g] = whole
        hi = before.astype(BF16)
        lo = (before - hi.astype(F32)).astype(BF16)
        q = grouped(lq, g)
        full = raw[g] + dot(jnp.concatenate([q, q], axis=1), jnp.concatenate([hi, lo], axis=0))
        inv = lax.rsqrt(jnp.mean(full * full, axis=-1, keepdims=True) + 1e-6)
        full = full * inv
        for i in range(group):
            h = g * group + i
            hs = slice(h * width, (h + 1) * width)
            o = (full[i * T2:(i + 1) * T2] * gain[pl.ds(r * (G * group) + h, 1), :]).astype(BF16)
            ob[:, hs] = o
            qs[g, i * T2:(i + 1) * T2, :] = (sq[:, hs].astype(F32) + o.astype(F32)).astype(BF16)

    def outgo(i, src, dst):
        return (remote(src[1], dst, out_s.at[i], out_r.at[i], sib),
                pltpu.make_async_copy(src[0], dst, out_l.at[i]))

    sends = [
        outgo(0, (ob.at[rows(r)], ob.at[rows(1 - r)]), lo_o.at[:, cols(r, QW)]),
        outgo(1, (total, total), st_o.at[pl.ds(r * G, G)]),
    ]
    for cp, lc in sends:
        cp.start()
        lc.start()

    scale = width ** (-0.5) * LOG2E
    ones = jnp.ones((T2, width), BF16)

    for lc in own:
        lc.wait()
    soft_wait(sib)
    mine = pl.ds(pl.multiple_of(c * T2, T2), T2)
    for g in range(G):
        s = slice(g * width, (g + 1) * width)
        sc = jnp.where(keep, dot(qs[g], sk[mine, s], ((1,), (1,))) * scale, -1e30)
        m = jnp.max(sc, axis=-1, keepdims=True)
        e = jnp.exp2(sc - m).astype(BF16)
        acc[g] = dot(e, jnp.concatenate([sv[mine, s], ones], axis=1))
        top[g] = jnp.broadcast_to(m, (R, width))

    def block(j, _):
        p = c - j
        soft_wait(2 * p)
        soft_wait(2 * p + 1)
        at = pl.ds(pl.multiple_of(p * T2, T2), T2)
        parts = [slice(g * width, (g + 1) * width) for g in range(G)]
        scs = [dot(qs[g], sk[at, s], ((1,), (1,))) * scale for g, s in enumerate(parts)]
        olds = [top[g] for g in range(G)]
        ms = [jnp.maximum(old, jnp.max(sc, axis=-1, keepdims=True)) for old, sc in zip(olds, scs)]
        es = [jnp.exp2(sc - m[:, 0:1]).astype(BF16)
              for sc, m in zip(scs, ms)]
        for g, s in enumerate(parts):
            new = dot(es[g], jnp.concatenate([sv[at, s], ones], axis=1))
            fade = jnp.exp2(olds[g] - ms[g])
            acc[g] = acc[g] * jnp.concatenate([fade, fade], axis=1) + new
            top[g] = ms[g]
        return 0

    lax.fori_loop(1, c + 1, block, 0)
    for g in range(G):
        o = (acc[g, :, 0:width] / acc[g, :, width:2 * width]).astype(BF16)
        for i in range(group):
            h = g * group + i
            out[:, h * width:(h + 1) * width] = o[i * T2:(i + 1) * T2]
    sends.append(outgo(2, (out.at[rows(r)], out.at[rows(1 - r)]), so_o.at[:, cols(r, QW)]))
    sends[2][0].start()
    sends[2][1].start()

    for cp, _, _ in pair:
        cp.wait_send()
    for a in range(2):
        soft_send(a, sib, 0).wait_send()
    for k in range(1, chips):
        state_send(k).wait_send()

        @pl.when(c + k < chips)
        def _():
            for h in range(2):
                for a in range(2):
                    soft_send(a, 2 * (c + k) + h, h).wait_send()
    other = 1 - r
    lands = (lo_o.at[:, cols(other, QW)], st_o.at[pl.ds(other * G, G)], so_o.at[:, cols(other, QW)])
    for i, (cp, lc) in enumerate(sends):
        cp.wait_send()
        lc.wait()
        src = (ob.at[rows(r)], total, out.at[rows(r)])[i]
        remote(src, lands[i], out_s.at[i], out_r.at[i], sib).wait_recv()


def deliver(a, b, c, a_o, b_o, c_o):
    a_o[...] = a[...]
    b_o[...] = b[...]
    c_o[...] = c[...]


def shards(n, lin_query, lin_keys, lin_values, state_in, norm_gain, soft_query, soft_keys, soft_values):
    T, D = lin_query.shape
    kvh, width, _ = state_in.shape
    kvd = lin_keys.shape[1]
    heads = D // width
    group = heads // kvh
    G = kvh // 2
    R = group * 2 * T
    chips = n // 2
    hbm = pl.BlockSpec(memory_space=pltpu.HBM)
    near = pl.BlockSpec(memory_space=pl.ANY)
    dma = pltpu.SemaphoreType.DMA
    shapes = (
        jax.ShapeDtypeStruct((T, D), BF16),
        jax.ShapeDtypeStruct(state_in.shape, F32),
        jax.ShapeDtypeStruct((T, D), BF16),
    )
    results = pl.pallas_call(
        functools.partial(kernel, n, group, width),
        out_shape=shapes,
        in_specs=[hbm] * 8,
        out_specs=(near, near, near),
        scratch_shapes=[
            pltpu.VMEM((2 * T, D // 2), BF16),
            pltpu.VMEM((2 * T, kvd // 2), BF16),
            pltpu.VMEM((2 * T, kvd // 2), BF16),
            pltpu.VMEM((2 * T, D // 2), BF16),
            pltpu.VMEM((n * T, kvd // 2), BF16),
            pltpu.VMEM((n * T, kvd // 2), BF16),
            pltpu.VMEM((heads, width), F32),
            pltpu.VMEM((G, width, width), F32),
            pltpu.VMEM((chips, G, width, width), BF16),
            pltpu.VMEM((G, width, width), F32),
            pltpu.VMEM((G, R, width), F32),
            pltpu.VMEM((G, R, width), BF16),
            pltpu.VMEM((2 * T, D // 2), BF16),
            pltpu.VMEM((2 * T, D // 2), BF16),
            pltpu.VMEM((G, R, width), F32),
            pltpu.VMEM((G, R, 2 * width), F32),
            dma((8,)), dma((4,)), dma((4,)), dma((2, n)), dma((2, n)),
            dma((chips,)), dma((chips,)), dma((3,)), dma((3,)), dma((3,)),
        ],
        compiler_params=pltpu.CompilerParams(
            collective_id=0, has_side_effects=True, vmem_limit_bytes=63 * 1024 * 1024),
        cost_estimate=pl.CostEstimate(flops=2_000_000_000, bytes_accessed=8_000_000, transcendentals=1_000_000),
    )(lin_query, lin_keys, lin_values, state_in, norm_gain.reshape(heads, width),
      soft_query, soft_keys, soft_values)
    return pl.pallas_call(
        deliver, out_shape=shapes,
    )(*results)


def solution(mesh):
    tok = P(("seq", "ctx"), None)
    st = P("seq", None, None)
    return jax.shard_map(
        functools.partial(shards, mesh.shape["ctx"]), mesh=mesh,
        in_specs=(tok, tok, tok, st, P(), tok, tok, tok),
        out_specs=(tok, st, tok), check_vma=False)
```

```python
import functools

import jax
import jax.numpy as jnp
from jax import lax
from jax.experimental import pallas as pl
from jax.experimental.pallas import tpu as pltpu
from jax.sharding import PartitionSpec as P

F32 = jnp.float32
BF16 = jnp.bfloat16
LOG2E = 1.4426950408889634


def dot(a, b, dims=((1,), (0,))):
    return lax.dot_general(a, b, (dims, ((), ())), preferred_element_type=F32)


def kernel(
    n, group, width,
    lq_h, lk_h, lv_h, st_h, gain_h, sq_h, sk_h, sv_h,
    lo_o, st_o, so_o,
    lq, lk, lv, sq, sk, sv, gain, stin, stall, total, raw, qs, ob, out, top, acc,
    loc, pair_s, pair_r, soft_s, soft_r, st_s, st_r, out_s, out_r, out_l,
):
    me = lax.axis_index("ctx")
    c, r = me // 2, me % 2
    sib = 2 * c + 1 - r
    chips = n // 2
    T = lk_h.shape[0]
    T2 = 2 * T
    KW = lk.shape[1]
    QW = lq.shape[1]
    G = KW // width
    R = group * T2

    def rows(d):
        return pl.ds(pl.multiple_of(d * T, T), T)

    def cols(h, w):
        return pl.ds(pl.multiple_of(h * w, w), w)

    def remote(src, dst, ss, rs, dev):
        return pltpu.make_async_remote_copy(
            src_ref=src, dst_ref=dst, send_sem=ss, recv_sem=rs,
            device_id={"ctx": dev}, device_id_type=pl.DeviceIdType.MESH)

    streams = ((lk_h, lk, KW), (lv_h, lv, KW), (lq_h, lq, QW), (sq_h, sq, QW))
    softs = ((sk_h, sk), (sv_h, sv))
    near = [pltpu.make_async_copy(src.at[:, cols(r, w)], dst.at[rows(r)], loc.at[i])
            for i, (src, dst, w) in enumerate(streams)]
    own = [pltpu.make_async_copy(src.at[:, cols(r, KW)], dst.at[rows(me)], loc.at[5 + a])
           for a, (src, dst) in enumerate(softs)]
    lst = pltpu.make_async_copy(st_h.at[pl.ds(r * G, G)], stin, loc.at[4])
    lgain = pltpu.make_async_copy(gain_h, gain, loc.at[7])
    for lc in near + own + [lst, lgain]:
        lc.start()

    barrier = pltpu.get_barrier_semaphore()
    for k in range(1, n):
        pl.semaphore_signal(barrier, inc=1, device_id={"ctx": lax.rem(me + k, n)},
                            device_id_type=pl.DeviceIdType.MESH)
    pl.semaphore_wait(barrier, n - 1)

    pair = []
    for i, (src, dst, w) in enumerate(streams):
        cp = remote(src.at[:, cols(1 - r, w)], dst.at[rows(r)], pair_s.at[i], pair_r.at[i], sib)
        cp.start()
        rc = remote(src.at[:, cols(r, w)], dst.at[rows(1 - r)], pair_s.at[i], pair_r.at[i], sib)
        pair.append((cp, near[i], rc))

    for a, (src, dst) in enumerate(softs):
        cp = remote(src.at[:, cols(1 - r, KW)], dst.at[rows(me)], soft_s.at[a, sib], soft_r.at[a, me], sib)
        cp.start()

    def soft_send(a, dest, h):
        src, dst = softs[a]
        return remote(src.at[:, h * KW:(h + 1) * KW], dst.at[rows(me)], soft_s.at[a, dest],
                      soft_r.at[a, me], dest)

    def soft_wait(d):
        for a, (src, dst) in enumerate(softs):
            remote(src.at[:, 0:KW], dst.at[rows(d)], soft_s.at[a, d], soft_r.at[a, d], sib).wait_recv()

    for i in range(2):
        pair[i][1].wait()
        pair[i][2].wait_recv()
    for g in range(G):
        s = slice(g * width, (g + 1) * width)
        stall[c, g] = dot(lk[:, s], lv[:, s], ((0,), (0,))).astype(BF16)

    def state_send(k):
        p = lax.rem(c + k, chips)
        return remote(stall.at[c], stall.at[c], st_s.at[p], st_r.at[c], 2 * p + r)

    def state_recv(k):
        p = lax.rem(c + k, chips)
        return remote(stall.at[p], stall.at[p], st_s.at[p], st_r.at[p], 2 * p + r)

    for k in range(1, chips):
        state_send(k).start()
    for k in range(1, chips):
        @pl.when(c + k < chips)
        def _():
            for h in range(2):
                for a in range(2):
                    soft_send(a, 2 * (c + k) + h, h).start()

    for i in range(2, 4):
        pair[i][1].wait()
        pair[i][2].wait_recv()
    tok = lax.rem(lax.broadcasted_iota(jnp.int32, (R, T2), 0), T2)
    keep = lax.broadcasted_iota(jnp.int32, (R, T2), 1) <= tok

    def grouped(ref, g):
        return jnp.concatenate(
            [ref[:, (g * group + i) * width:(g * group + i + 1) * width] for i in range(group)], axis=0)

    for g in range(G):
        s = slice(g * width, (g + 1) * width)
        sc = jnp.where(keep, dot(grouped(lq, g), lk[:, s], ((1,), (1,))), 0.0)
        hi = sc.astype(BF16)
        lo = (sc - hi.astype(F32)).astype(BF16)
        raw[g] = dot(jnp.concatenate([hi, lo], axis=1), jnp.concatenate([lv[:, s], lv[:, s]], axis=0))

    lst.wait()
    lgain.wait()
    for k in range(1, chips):
        state_recv(k).wait_recv()
    for g in range(G):
        before = stin[g]
        whole = before
        for p in range(chips):
            x = stall[p, g].astype(F32)
            whole = whole + x
            before = before + jnp.where(p < c, x, 0.0)
        total[g] = whole
        hi = before.astype(BF16)
        lo = (before - hi.astype(F32)).astype(BF16)
        q = grouped(lq, g)
        full = raw[g] + dot(jnp.concatenate([q, q], axis=1), jnp.concatenate([hi, lo], axis=0))
        inv = lax.rsqrt(jnp.mean(full * full, axis=-1, keepdims=True) + 1e-6)
        full = full * inv
        for i in range(group):
            h = g * group + i
            hs = slice(h * width, (h + 1) * width)
            o = (full[i * T2:(i + 1) * T2] * gain[pl.ds(r * (G * group) + h, 1), :]).astype(BF16)
            ob[:, hs] = o
            qs[g, i * T2:(i + 1) * T2, :] = (sq[:, hs].astype(F32) + o.astype(F32)).astype(BF16)

    def outgo(i, src, dst):
        return (remote(src[1], dst, out_s.at[i], out_r.at[i], sib),
                pltpu.make_async_copy(src[0], dst, out_l.at[i]))

    sends = [
        outgo(0, (ob.at[rows(r)], ob.at[rows(1 - r)]), lo_o.at[:, cols(r, QW)]),
        outgo(1, (total, total), st_o.at[pl.ds(r * G, G)]),
    ]
    for cp, lc in sends:
        cp.start()
        lc.start()

    scale = width ** (-0.5) * LOG2E
    ones = jnp.ones((T2, width), BF16)

    for lc in own:
        lc.wait()
    soft_wait(sib)
    mine = pl.ds(pl.multiple_of(c * T2, T2), T2)
    for g in range(G):
        s = slice(g * width, (g + 1) * width)
        sc = jnp.where(keep, dot(qs[g], sk[mine, s], ((1,), (1,))) * scale, -1e30)
        m = jnp.max(sc, axis=-1, keepdims=True)
        e = jnp.exp2(sc - m).astype(BF16)
        acc[g] = dot(e, jnp.concatenate([sv[mine, s], ones], axis=1))
        top[g] = jnp.broadcast_to(m, (R, width))

    def block(j, _):
        p = c - j
        soft_wait(2 * p)
        soft_wait(2 * p + 1)
        at = pl.ds(pl.multiple_of(p * T2, T2), T2)
        parts = [slice(g * width, (g + 1) * width) for g in range(G)]
        scs = [dot(qs[g], sk[at, s], ((1,), (1,))) * scale for g, s in enumerate(parts)]
        olds = [top[g] for g in range(G)]
        ms = [jnp.maximum(old, jnp.max(sc, axis=-1, keepdims=True)) for old, sc in zip(olds, scs)]
        es = [jnp.exp2(sc - m[:, 0:1]).astype(BF16)
              for sc, m in zip(scs, ms)]
        for g, s in enumerate(parts):
            new = dot(es[g], jnp.concatenate([sv[at, s], ones], axis=1))
            fade = jnp.exp2(olds[g] - ms[g])
            acc[g] = acc[g] * jnp.concatenate([fade, fade], axis=1) + new
            top[g] = ms[g]
        return 0

    lax.fori_loop(1, c + 1, block, 0)
    for g in range(G):
        o = (acc[g, :, 0:width] / acc[g, :, width:2 * width]).astype(BF16)
        for i in range(group):
            h = g * group + i
            out[:, h * width:(h + 1) * width] = o[i * T2:(i + 1) * T2]
    sends.append(outgo(2, (out.at[rows(r)], out.at[rows(1 - r)]), so_o.at[:, cols(r, QW)]))
    sends[2][0].start()
    sends[2][1].start()

    for cp, _, _ in pair:
        cp.wait_send()
    for a in range(2):
        soft_send(a, sib, 0).wait_send()
    for k in range(1, chips):
        state_send(k).wait_send()

        @pl.when(c + k < chips)
        def _():
            for h in range(2):
                for a in range(2):
                    soft_send(a, 2 * (c + k) + h, h).wait_send()
    other = 1 - r
    lands = (lo_o.at[:, cols(other, QW)], st_o.at[pl.ds(other * G, G)], so_o.at[:, cols(other, QW)])
    for i, (cp, lc) in enumerate(sends):
        cp.wait_send()
        lc.wait()
        src = (ob.at[rows(r)], total, out.at[rows(r)])[i]
        remote(src, lands[i], out_s.at[i], out_r.at[i], sib).wait_recv()


def deliver(a, b, c, a_o, b_o, c_o, a_v, b_v, c_v, sem, sem_o):
    trips = [
        (pltpu.make_async_copy(x, v, sem.at[i]), pltpu.make_async_copy(v, y, sem_o.at[i]))
        for i, (x, v, y) in enumerate(((a, a_v, a_o), (b, b_v, b_o), (c, c_v, c_o)))
    ]
    for get, _ in trips:
        get.start()
    for get, put in trips:
        get.wait()
        put.start()
    for _, put in trips:
        put.wait()


def shards(n, lin_query, lin_keys, lin_values, state_in, norm_gain, soft_query, soft_keys, soft_values):
    T, D = lin_query.shape
    kvh, width, _ = state_in.shape
    kvd = lin_keys.shape[1]
    heads = D // width
    group = heads // kvh
    G = kvh // 2
    R = group * 2 * T
    chips = n // 2
    hbm = pl.BlockSpec(memory_space=pltpu.HBM)
    near = pl.BlockSpec(memory_space=pl.ANY)
    dma = pltpu.SemaphoreType.DMA
    shapes = (
        jax.ShapeDtypeStruct((T, D), BF16),
        jax.ShapeDtypeStruct(state_in.shape, F32),
        jax.ShapeDtypeStruct((T, D), BF16),
    )
    results = pl.pallas_call(
        functools.partial(kernel, n, group, width),
        out_shape=shapes,
        in_specs=[hbm] * 8,
        out_specs=(near, near, near),
        scratch_shapes=[
            pltpu.VMEM((2 * T, D // 2), BF16),
            pltpu.VMEM((2 * T, kvd // 2), BF16),
            pltpu.VMEM((2 * T, kvd // 2), BF16),
            pltpu.VMEM((2 * T, D // 2), BF16),
            pltpu.VMEM((n * T, kvd // 2), BF16),
            pltpu.VMEM((n * T, kvd // 2), BF16),
            pltpu.VMEM((heads, width), F32),
            pltpu.VMEM((G, width, width), F32),
            pltpu.VMEM((chips, G, width, width), BF16),
            pltpu.VMEM((G, width, width), F32),
            pltpu.VMEM((G, R, width), F32),
            pltpu.VMEM((G, R, width), BF16),
            pltpu.VMEM((2 * T, D // 2), BF16),
            pltpu.VMEM((2 * T, D // 2), BF16),
            pltpu.VMEM((G, R, width), F32),
            pltpu.VMEM((G, R, 2 * width), F32),
            dma((8,)), dma((4,)), dma((4,)), dma((2, n)), dma((2, n)),
            dma((chips,)), dma((chips,)), dma((3,)), dma((3,)), dma((3,)),
        ],
        compiler_params=pltpu.CompilerParams(
            collective_id=0, has_side_effects=True, vmem_limit_bytes=63 * 1024 * 1024),
        cost_estimate=pl.CostEstimate(flops=2_000_000_000, bytes_accessed=8_000_000, transcendentals=1_000_000),
    )(lin_query, lin_keys, lin_values, state_in, norm_gain.reshape(heads, width),
      soft_query, soft_keys, soft_values)
    return pl.pallas_call(
        deliver, out_shape=shapes, in_specs=[hbm] * 3, out_specs=(hbm,) * 3,
        scratch_shapes=[pltpu.VMEM(x.shape, x.dtype) for x in shapes] + [dma((3,)), dma((3,))],
        compiler_params=pltpu.CompilerParams(vmem_limit_bytes=63 * 1024 * 1024),
    )(*results)


def solution(mesh):
    tok = P(("seq", "ctx"), None)
    st = P("seq", None, None)
    return jax.shard_map(
        functools.partial(shards, mesh.shape["ctx"]), mesh=mesh,
        in_specs=(tok, tok, tok, st, P(), tok, tok, tok),
        out_specs=(tok, st, tok), check_vma=False)
```

```python
import functools

import jax
import jax.numpy as jnp
from jax import lax
from jax.experimental import pallas as pl
from jax.experimental.pallas import tpu as pltpu
from jax.sharding import PartitionSpec as P

F32 = jnp.float32
BF16 = jnp.bfloat16
LOG2E = 1.4426950408889634


def dot(a, b, dims=((1,), (0,))):
    return lax.dot_general(a, b, (dims, ((), ())), preferred_element_type=F32)


def kernel(
    n, group, width,
    lq_h, lk_h, lv_h, st_h, gain_h, sq_h, sk_h, sv_h,
    lo_o, st_o, so_o,
    lq, lk, lv, sq, sk, sv, gain, stin, stall, total, raw, qs, ob, out, top, acc,
    loc, pair_s, pair_r, soft_s, soft_r, st_s, st_r, out_s, out_r, out_l,
):
    me = lax.axis_index("ctx")
    c, r = me // 2, me % 2
    sib = 2 * c + 1 - r
    chips = n // 2
    T = lk_h.shape[0]
    T2 = 2 * T
    KW = lk.shape[1]
    QW = lq.shape[1]
    G = KW // width
    R = group * T2

    def rows(d):
        return pl.ds(pl.multiple_of(d * T, T), T)

    def cols(h, w):
        return pl.ds(pl.multiple_of(h * w, w), w)

    def remote(src, dst, ss, rs, dev):
        return pltpu.make_async_remote_copy(
            src_ref=src, dst_ref=dst, send_sem=ss, recv_sem=rs,
            device_id={"ctx": dev}, device_id_type=pl.DeviceIdType.MESH)

    streams = ((lk_h, lk, KW), (lv_h, lv, KW), (lq_h, lq, QW), (sq_h, sq, QW))
    softs = ((sk_h, sk), (sv_h, sv))
    near = [pltpu.make_async_copy(src.at[:, cols(r, w)], dst.at[rows(r)], loc.at[i])
            for i, (src, dst, w) in enumerate(streams)]
    own = [pltpu.make_async_copy(src.at[:, cols(r, KW)], dst.at[rows(me)], loc.at[5 + a])
           for a, (src, dst) in enumerate(softs)]
    lst = pltpu.make_async_copy(st_h.at[pl.ds(r * G, G)], stin, loc.at[4])
    lgain = pltpu.make_async_copy(gain_h, gain, loc.at[7])
    for lc in near + own + [lst, lgain]:
        lc.start()

    barrier = pltpu.get_barrier_semaphore()
    for k in range(1, n):
        pl.semaphore_signal(barrier, inc=1, device_id={"ctx": lax.rem(me + k, n)},
                            device_id_type=pl.DeviceIdType.MESH)
    pl.semaphore_wait(barrier, n - 1)

    pair = []
    for i, (src, dst, w) in enumerate(streams):
        cp = remote(src.at[:, cols(1 - r, w)], dst.at[rows(r)], pair_s.at[i], pair_r.at[i], sib)
        cp.start()
        rc = remote(src.at[:, cols(r, w)], dst.at[rows(1 - r)], pair_s.at[i], pair_r.at[i], sib)
        pair.append((cp, near[i], rc))

    for a, (src, dst) in enumerate(softs):
        cp = remote(src.at[:, cols(1 - r, KW)], dst.at[rows(me)], soft_s.at[a, sib], soft_r.at[a, me], sib)
        cp.start()

    def soft_send(a, dest, h):
        src, dst = softs[a]
        return remote(src.at[:, h * KW:(h + 1) * KW], dst.at[rows(me)], soft_s.at[a, dest],
                      soft_r.at[a, me], dest)

    def soft_wait(d):
        for a, (src, dst) in enumerate(softs):
            remote(src.at[:, 0:KW], dst.at[rows(d)], soft_s.at[a, d], soft_r.at[a, d], sib).wait_recv()

    for i in range(2):
        pair[i][1].wait()
        pair[i][2].wait_recv()
    for g in range(G):
        s = slice(g * width, (g + 1) * width)
        stall[c, g] = dot(lk[:, s], lv[:, s], ((0,), (0,))).astype(BF16)

    def state_send(k):
        p = lax.rem(c + k, chips)
        return remote(stall.at[c], stall.at[c], st_s.at[p], st_r.at[c], 2 * p + r)

    def state_recv(k):
        p = lax.rem(c + k, chips)
        return remote(stall.at[p], stall.at[p], st_s.at[p], st_r.at[p], 2 * p + r)

    for k in range(1, chips):
        state_send(k).start()
    for k in range(1, chips):
        @pl.when(c + k < chips)
        def _():
            for h in range(2):
                for a in range(2):
                    soft_send(a, 2 * (c + k) + h, h).start()

    for i in range(2, 4):
        pair[i][1].wait()
        pair[i][2].wait_recv()
    tok = lax.rem(lax.broadcasted_iota(jnp.int32, (R, T2), 0), T2)
    keep = lax.broadcasted_iota(jnp.int32, (R, T2), 1) <= tok

    def grouped(ref, g):
        return jnp.concatenate(
            [ref[:, (g * group + i) * width:(g * group + i + 1) * width] for i in range(group)], axis=0)

    for g in range(G):
        s = slice(g * width, (g + 1) * width)
        sc = jnp.where(keep, dot(grouped(lq, g), lk[:, s], ((1,), (1,))), 0.0)
        hi = sc.astype(BF16)
        lo = (sc - hi.astype(F32)).astype(BF16)
        raw[g] = dot(jnp.concatenate([hi, lo], axis=1), jnp.concatenate([lv[:, s], lv[:, s]], axis=0))

    lst.wait()
    lgain.wait()
    for k in range(1, chips):
        state_recv(k).wait_recv()
    for g in range(G):
        before = stin[g]
        whole = before
        for p in range(chips):
            x = stall[p, g].astype(F32)
            whole = whole + x
            before = before + jnp.where(p < c, x, 0.0)
        total[g] = whole
        hi = before.astype(BF16)
        lo = (before - hi.astype(F32)).astype(BF16)
        q = grouped(lq, g)
        full = raw[g] + dot(jnp.concatenate([q, q], axis=1), jnp.concatenate([hi, lo], axis=0))
        inv = lax.rsqrt(jnp.mean(full * full, axis=-1, keepdims=True) + 1e-6)
        full = full * inv
        for i in range(group):
            h = g * group + i
            hs = slice(h * width, (h + 1) * width)
            o = (full[i * T2:(i + 1) * T2] * gain[pl.ds(r * (G * group) + h, 1), :]).astype(BF16)
            ob[:, hs] = o
            qs[g, i * T2:(i + 1) * T2, :] = (sq[:, hs].astype(F32) + o.astype(F32)).astype(BF16)

    def outgo(i, src, dst):
        return (remote(src[1], dst, out_s.at[i], out_r.at[i], sib),
                pltpu.make_async_copy(src[0], dst, out_l.at[i]))

    sends = [
        outgo(0, (ob.at[rows(r)], ob.at[rows(1 - r)]), lo_o.at[:, cols(r, QW)]),
        outgo(1, (total, total), st_o.at[pl.ds(r * G, G)]),
    ]
    for cp, lc in sends:
        cp.start()
        lc.start()

    scale = width ** (-0.5) * LOG2E
    ones = jnp.ones((T2, width), BF16)

    for lc in own:
        lc.wait()
    soft_wait(sib)
    mine = pl.ds(pl.multiple_of(c * T2, T2), T2)
    heads = [slice(g * width, (g + 1) * width) for g in range(G)]
    first = [jnp.where(keep, dot(qs[g], sk[mine, s], ((1,), (1,))) * scale, -1e30) for g, s in enumerate(heads)]
    tops = [jnp.max(sc, axis=-1, keepdims=True) for sc in first]
    exps = [jnp.exp2(sc - m).astype(BF16) for sc, m in zip(first, tops)]
    for g, s in enumerate(heads):
        acc[g] = dot(exps[g], jnp.concatenate([sv[mine, s], ones], axis=1))
        top[g] = jnp.broadcast_to(tops[g], (R, width))

    def block(j, _):
        p = c - j
        soft_wait(2 * p)
        soft_wait(2 * p + 1)
        at = pl.ds(pl.multiple_of(p * T2, T2), T2)
        parts = [slice(g * width, (g + 1) * width) for g in range(G)]
        scs = [dot(qs[g], sk[at, s], ((1,), (1,))) * scale for g, s in enumerate(parts)]
        olds = [top[g] for g in range(G)]
        ms = [jnp.maximum(old, jnp.max(sc, axis=-1, keepdims=True)) for old, sc in zip(olds, scs)]
        es = [jnp.exp2(sc - m[:, 0:1]).astype(BF16)
              for sc, m in zip(scs, ms)]
        for g, s in enumerate(parts):
            new = dot(es[g], jnp.concatenate([sv[at, s], ones], axis=1))
            fade = jnp.exp2(olds[g] - ms[g])
            acc[g] = acc[g] * jnp.concatenate([fade, fade], axis=1) + new
            top[g] = ms[g]
        return 0

    lax.fori_loop(1, c + 1, block, 0)
    for g in range(G):
        o = (acc[g, :, 0:width] / acc[g, :, width:2 * width]).astype(BF16)
        for i in range(group):
            h = g * group + i
            out[:, h * width:(h + 1) * width] = o[i * T2:(i + 1) * T2]
    sends.append(outgo(2, (out.at[rows(r)], out.at[rows(1 - r)]), so_o.at[:, cols(r, QW)]))
    sends[2][0].start()
    sends[2][1].start()

    for cp, _, _ in pair:
        cp.wait_send()
    for a in range(2):
        soft_send(a, sib, 0).wait_send()
    for k in range(1, chips):
        state_send(k).wait_send()

        @pl.when(c + k < chips)
        def _():
            for h in range(2):
                for a in range(2):
                    soft_send(a, 2 * (c + k) + h, h).wait_send()
    other = 1 - r
    lands = (lo_o.at[:, cols(other, QW)], st_o.at[pl.ds(other * G, G)], so_o.at[:, cols(other, QW)])
    for i, (cp, lc) in enumerate(sends):
        cp.wait_send()
        lc.wait()
        src = (ob.at[rows(r)], total, out.at[rows(r)])[i]
        remote(src, lands[i], out_s.at[i], out_r.at[i], sib).wait_recv()


def deliver(a, b, c, a_o, b_o, c_o, a_v, b_v, c_v, sem, sem_o):
    trips = [
        (pltpu.make_async_copy(x, v, sem.at[i]), pltpu.make_async_copy(v, y, sem_o.at[i]))
        for i, (x, v, y) in enumerate(((a, a_v, a_o), (b, b_v, b_o), (c, c_v, c_o)))
    ]
    for get, _ in trips:
        get.start()
    for get, put in trips:
        get.wait()
        put.start()
    for _, put in trips:
        put.wait()


def shards(n, lin_query, lin_keys, lin_values, state_in, norm_gain, soft_query, soft_keys, soft_values):
    T, D = lin_query.shape
    kvh, width, _ = state_in.shape
    kvd = lin_keys.shape[1]
    heads = D // width
    group = heads // kvh
    G = kvh // 2
    R = group * 2 * T
    chips = n // 2
    hbm = pl.BlockSpec(memory_space=pltpu.HBM)
    near = pl.BlockSpec(memory_space=pl.ANY)
    dma = pltpu.SemaphoreType.DMA
    shapes = (
        jax.ShapeDtypeStruct((T, D), BF16),
        jax.ShapeDtypeStruct(state_in.shape, F32),
        jax.ShapeDtypeStruct((T, D), BF16),
    )
    results = pl.pallas_call(
        functools.partial(kernel, n, group, width),
        out_shape=shapes,
        in_specs=[hbm] * 8,
        out_specs=(near, near, near),
        scratch_shapes=[
            pltpu.VMEM((2 * T, D // 2), BF16),
            pltpu.VMEM((2 * T, kvd // 2), BF16),
            pltpu.VMEM((2 * T, kvd // 2), BF16),
            pltpu.VMEM((2 * T, D // 2), BF16),
            pltpu.VMEM((n * T, kvd // 2), BF16),
            pltpu.VMEM((n * T, kvd // 2), BF16),
            pltpu.VMEM((heads, width), F32),
            pltpu.VMEM((G, width, width), F32),
            pltpu.VMEM((chips, G, width, width), BF16),
            pltpu.VMEM((G, width, width), F32),
            pltpu.VMEM((G, R, width), F32),
            pltpu.VMEM((G, R, width), BF16),
            pltpu.VMEM((2 * T, D // 2), BF16),
            pltpu.VMEM((2 * T, D // 2), BF16),
            pltpu.VMEM((G, R, width), F32),
            pltpu.VMEM((G, R, 2 * width), F32),
            dma((8,)), dma((4,)), dma((4,)), dma((2, n)), dma((2, n)),
            dma((chips,)), dma((chips,)), dma((3,)), dma((3,)), dma((3,)),
        ],
        compiler_params=pltpu.CompilerParams(
            collective_id=0, has_side_effects=True, vmem_limit_bytes=63 * 1024 * 1024),
        cost_estimate=pl.CostEstimate(flops=2_000_000_000, bytes_accessed=8_000_000, transcendentals=1_000_000),
    )(lin_query, lin_keys, lin_values, state_in, norm_gain.reshape(heads, width),
      soft_query, soft_keys, soft_values)
    return pl.pallas_call(
        deliver, out_shape=shapes, in_specs=[hbm] * 3, out_specs=(hbm,) * 3,
        scratch_shapes=[pltpu.VMEM(x.shape, x.dtype) for x in shapes] + [dma((3,)), dma((3,))],
        compiler_params=pltpu.CompilerParams(vmem_limit_bytes=63 * 1024 * 1024),
    )(*results)


def solution(mesh):
    tok = P(("seq", "ctx"), None)
    st = P("seq", None, None)
    return jax.shard_map(
        functools.partial(shards, mesh.shape["ctx"]), mesh=mesh,
        in_specs=(tok, tok, tok, st, P(), tok, tok, tok),
        out_specs=(tok, st, tok), check_vma=False)
```
